32 devices in a mesh: blk: 4 (over x, core), grp: 8 (over z, y).
Axes of the slice: x: 2, y: 2, z: 4, core: 2. Of those that a mesh axis runs over, the one named last changes fastest.
Arguments:
- table: bfloat16 [65536, 512], P(('blk', 'grp')), may hold values from -6 to 6
- row_ids: int32 [4096], P(('blk', 'grp')), may hold values from 0 to 2047
- potentials: bfloat16 [4096], P(('blk', 'grp')), may hold values from -1 to 6
- centroids: bfloat16 [65536, 512], P(('blk', 'grp')), may hold values from -30 to 30
- balance: float32 [65536], P(('blk', 'grp')), may hold values from 0.001 to 1
Outputs:
- new_centroids: float32 [65536, 512], P(('blk', 'grp'))
- column_potential: float32 [65536], P(('blk', 'grp'))
The draws below stay inside these ranges and needn't reach their ends.
Inputs may be any that keep to these rules, and one draw needn't show every extreme that they name: `row_ids`: offsets into the records held by the row's own device.
All inputs are finite; a program needn't handle non-finite values.
Results may differ from the reference program's by a relative error of at most 0.0027.
Values may be sent and summed in bfloat16 or wider, within the bound.
No kernel may reach another device: no remote copies, remote signals or barrier semaphores. Data moves between devices by JAX's collectives and lax.ppermute only.
A program may use at most 128 MiB of HBM per device.

```python
import math
import jax
import jax.numpy as jnp
from jax import lax

D = 512
K = 65536
ROWS_DEV = 128
TABLE_DEV = 2048
ROWS = 4096
TABLE = 65536


def draw_table(key, part):
    first = jax.random.fold_in(key, 37)
    value = jnp.clip(jax.random.normal(first, (TABLE, D), jnp.float32), -6.0, 6.0)
    return value.astype(jnp.bfloat16)


def draw_potentials(key, part):
    first = jax.random.fold_in(jax.random.fold_in(key, 11), 0)
    value = jnp.clip(0.06 * jax.random.normal(first, (ROWS,), jnp.float32), -0.9, 0.9)
    return value.astype(jnp.bfloat16)


def draw_centroids(key, part):
    first = jax.random.fold_in(jax.random.fold_in(key, 23), 0)
    value = jnp.clip(jax.random.normal(first, (K, D), jnp.float32), -6.0, 6.0)
    return value.astype(jnp.bfloat16)


def with_ends(array, key, least, high):
    dims = array.shape
    spot = [jax.random.randint(jax.random.fold_in(key, axis), (), 0, dims[axis]) for axis in range(len(dims))]
    array = array.at[tuple(spot)].set(least)
    longest = dims.index(max(dims))
    spot[longest] = (spot[longest] + 1) % dims[longest]
    return array.at[tuple(spot)].set(high)


def shard_levels(own_key, dims, cuts, smallest, largest):
    loudness, own = 1.0, jax.random.fold_in(own_key, 6)
    for dim, shards_of in cuts:
        steps = jnp.exp(jax.random.uniform(jax.random.fold_in(own, dim), (shards_of,), jnp.float32, smallest / len(cuts), largest / len(cuts)))
        loudness = loudness * jnp.repeat(steps, dims[dim] // shards_of).reshape([-1 if axis == dim else 1 for axis in range(len(dims))])
    return loudness


def setup_inputs(seed: int = 0) -> dict:
    splits = jax.random.split(jax.random.key(seed), 6)
    return {
        "table": draw_table(jax.random.fold_in(splits[5], 71), 0),
        "row_ids": with_ends(jax.random.randint(splits[1], (ROWS,), 0, TABLE_DEV), jax.random.fold_in(splits[1], 1), 0, TABLE_DEV - 1).astype(jnp.int32),
        "potentials": draw_potentials(jax.random.fold_in(splits[5], 71), 0),
        "centroids": draw_centroids(jax.random.fold_in(splits[5], 71), 0),
        "balance": jnp.clip(jnp.exp(math.log(1.0) - 6.9077552 * jax.random.uniform(splits[4], (K,), jnp.float32) ** shard_levels(splits[4], (K,), ((0, 32),), -0.2, 0.2)), 0.001, 1.0),
    }


def column_scores(rows, pots, norms, panel, scale):
    inner = lax.dot_general(rows, panel, (((1,), (1,)), ((), ())), preferred_element_type=jnp.float32)
    centre = lax.optimization_barrier(jnp.sum(jnp.square(panel.astype(jnp.float32)), axis=1))
    cost = (norms[:, None] - 2.0 * inner + centre[None, :]) / rows.shape[1]
    return scale * (pots.astype(jnp.float32)[:, None] - cost)

def reference(table, row_ids, potentials, centroids, balance):
    scale = 1.5 * math.sqrt(D)
    owner = (jnp.arange(ROWS, dtype=jnp.int32) // ROWS_DEV).astype(jnp.int32)
    where = (owner * TABLE_DEV + row_ids).astype(jnp.int32)
    rows = table[where]
    norms = lax.optimization_barrier(jnp.sum(jnp.square(rows.astype(jnp.float32)), axis=1))
    blocks = centroids.reshape(K // 512, 512, D)
    masses = balance.reshape(K // 512, 512)

    def one_block(pair):
        panel, target = pair
        scores = column_scores(rows, potentials, norms, panel, scale)
        peak = lax.optimization_barrier(jnp.max(scores, axis=0))
        expd = jnp.exp(scores - peak[None, :])
        mass = lax.optimization_barrier(jnp.sum(expd, axis=0))
        weights = expd.astype(jnp.bfloat16)
        numer = lax.dot_general(weights, rows, (((0,), (0,)), ((), ())), preferred_element_type=jnp.float32)
        means = numer / mass[:, None]
        potential = (jnp.log(target) - peak - jnp.log(mass)) / scale
        return (means, potential)
    means, potential = lax.map(one_block, (blocks, masses))
    return (means.reshape(K, D), potential.reshape(K))
```

```python
import functools
import math

import jax
import jax.numpy as jnp
from jax import lax
from jax.experimental import pallas as pl
from jax.experimental.pallas import tpu as pltpu
from jax.sharding import PartitionSpec as P

BF16, F32 = jnp.bfloat16, jnp.float32
AXES = ("blk", "grp")
EXTRA = 16
LANES = 128
VMEM = pl.BlockSpec(memory_space=pltpu.VMEM)
NT = (((1,), (1,)), ((), ()))


def in_vmem(array):
    return pltpu.with_memory_space_constraint(array, pltpu.VMEM)


def eye():
    shape = (LANES, LANES)
    return lax.broadcasted_iota(jnp.int32, shape, 0) == lax.broadcasted_iota(jnp.int32, shape, 1)


def to_row(column):
    return jnp.sum(jnp.where(eye(), column, 0.0), axis=0, keepdims=True)


def to_column(row):
    return jnp.sum(jnp.where(eye(), row, 0.0), axis=1, keepdims=True)


def gather_kernel(table_ref, ids_ref, pots_ref, out_ref):
    records, width = table_ref.shape
    count = ids_ref.shape[1]
    step = 512
    column = to_column(ids_ref[...].astype(F32)).astype(jnp.int32)
    rows = jnp.zeros((count, width), F32)
    for first in range(0, records, step):
        spot = lax.broadcasted_iota(jnp.int32, (count, step), 1) + first
        pick = jnp.where(spot == column, 1.0, 0.0).astype(BF16)
        rows += jnp.dot(pick, table_ref[first : first + step, :], preferred_element_type=F32)
    norm = to_row(jnp.sum(jnp.square(rows), axis=1, keepdims=True))
    term = pots_ref[...].astype(F32) * (width / 2) - 0.5 * norm
    high = term.astype(BF16).astype(F32)
    middle = (term - high).astype(BF16).astype(F32)
    low = term - high - middle
    line = lax.broadcasted_iota(jnp.int32, (EXTRA, LANES), 0)
    parts = jnp.where(line == 0, high, jnp.where(line == 1, middle, jnp.where(line == 2, low, 0.0)))
    out_ref[0:count, :] = rows.astype(BF16)
    out_ref[count:, :] = jnp.zeros((EXTRA, width), BF16)
    out_ref[count:, 0:LANES] = parts.astype(BF16)


def gather(table, row_ids, potentials):
    count, width = row_ids.shape[0], table.shape[1]
    return pl.pallas_call(
        gather_kernel,
        out_shape=pltpu.VMEM((count + EXTRA, width), BF16),
        in_specs=[VMEM] * 3,
        out_specs=VMEM,
        compiler_params=pltpu.CompilerParams(vmem_limit_bytes=16 << 20),
        name="gather",
    )(table, row_ids.reshape(1, count), potentials.reshape(1, count))


def pieces(refs, count):
    rows, terms = [], []
    for ref in refs:
        for first in range(0, ref.shape[0], count + EXTRA):
            rows.append(ref[first : first + count, :])
            extra = ref[first + count : first + count + EXTRA, 0:LANES].astype(F32)
            terms.append(jnp.sum(extra, axis=0, keepdims=True))
    return rows, terms


def block_step(centres, rows, terms, alpha, old):
    shifted = lax.dot_general(centres, rows, NT, preferred_element_type=F32) + terms
    top = jnp.max(shifted, axis=1, keepdims=True)
    if old is not None:
        top = jnp.maximum(old[0], top)
    expd = jnp.exp2((shifted - top) * alpha)
    mass = expd[:, 0:LANES]
    for first in range(LANES, expd.shape[1], LANES):
        mass = mass + expd[:, first : first + LANES]
    numer = jnp.dot(expd.astype(BF16), rows, preferred_element_type=F32)
    if old is not None:
        shrink = jnp.exp2((old[0] - top) * alpha)
        mass = old[1] * shrink + mass
        numer = old[2] * shrink + numer
    return top, mass, numer


def visit_kernel(shards, count, block, chunk, first, last, scale, *refs):
    shard_refs, refs = refs[:shards], refs[shards:]
    centres_ref, refs = refs[0], refs[1:]
    state_in, refs = (None, refs) if first else (refs[:3], refs[3:])
    balance_ref, refs = (refs[0], refs[1:]) if last else (None, refs)
    width = centres_ref.shape[1]
    alpha = math.log2(math.e) * 2.0 * scale / width
    rows, terms = pieces(shard_refs, count)
    per = max(1, chunk // count)
    groups = [
        (jnp.concatenate(rows[i : i + per], axis=0), jnp.concatenate(terms[i : i + per], axis=1))
        for i in range(0, len(rows), per)
    ]

    def one(j, _):
        at = pl.ds(pl.multiple_of(j * block, block), block)
        centres = centres_ref[at, :]
        state = None if first else (state_in[0][at, 0:1], state_in[1][at, :], state_in[2][at, :])
        for group_rows, group_terms in groups:
            state = block_step(centres, group_rows, group_terms, alpha, state)
        top, mass, numer = state
        if not last:
            refs[0][at, :] = jnp.broadcast_to(top, (block, LANES))
            refs[1][at, :] = mass
            refs[2][at, :] = numer
            return 0
        means_ref, potential_ref = refs
        mass = jnp.sum(mass, axis=1, keepdims=True)
        means_ref[at, :] = numer / mass
        centre = jnp.sum(jnp.square(centres.astype(F32)), axis=1, keepdims=True)
        peak = (scale / width) * (2.0 * top - centre)
        for i in range(block // LANES):
            part = slice(i * LANES, (i + 1) * LANES)
            line = pl.ds(j * (block // LANES) + i, 1)
            potential_ref[line, :] = (
                jnp.log(balance_ref[line, :]) - to_row(peak[part]) - jnp.log(to_row(mass[part]))
            ) / scale
        return 0

    lax.fori_loop(0, centres_ref.shape[0] // block, one, 0)


def visit(shards, count, centroids, state, scale, balance=None, chunk=512):
    total, width = centroids.shape
    block = min(1024, total)
    first, last = state is None, balance is not None
    number = sum(s.shape[0] // (count + EXTRA) for s in shards)
    if last:
        out_shape = (
            jax.ShapeDtypeStruct((total, width), F32),
            jax.ShapeDtypeStruct((total // LANES, LANES), F32),
        )
    else:
        out_shape = (
            pltpu.VMEM((total, LANES), F32),
            pltpu.VMEM((total, LANES), F32),
            pltpu.VMEM((total, width), F32),
        )
    args = [in_vmem(s) for s in shards] + [in_vmem(centroids)]
    aliases = {}
    if not first:
        if not last:
            aliases = {len(args) + i: i for i in range(3)}
        args += [in_vmem(s) for s in state]
    if last:
        args.append(balance.reshape(total // LANES, LANES))
    rows = number * count
    return pl.pallas_call(
        functools.partial(visit_kernel, len(shards), count, block, chunk, first, last, scale),
        out_shape=out_shape,
        in_specs=[VMEM] * len(args),
        out_specs=tuple([VMEM] * len(out_shape)),
        input_output_aliases=aliases,
        compiler_params=pltpu.CompilerParams(vmem_limit_bytes=40 << 20),
        cost_estimate=pl.CostEstimate(
            flops=4 * rows * total * width, bytes_accessed=4 * total * width, transcendentals=rows * total
        ),
        name="visit",
    )(*args)


def pack(parts):
    return parts[0] if len(parts) == 1 else jnp.concatenate(parts, axis=0)


def body(table, row_ids, potentials, centroids, balance):
    scale = 1.5 * math.sqrt(table.shape[1])
    count = row_ids.shape[0]
    blk, grp = lax.axis_size("blk"), lax.axis_size("grp")

    def swap(array, flip):
        route = [(i, flip(i // grp, i % grp)) for i in range(blk * grp)]
        return lax.ppermute(array, AXES, route)

    def core(array):
        return swap(array, lambda b, g: (b ^ 1) * grp + g)

    def grp_bit(array, bit):
        return swap(array, lambda b, g: b * grp + (g ^ bit))

    def one_way(array):
        return swap(array, lambda b, g: b * grp + (g ^ 1) if b & 1 else (b ^ 2) * grp + g)

    def other_way(array):
        return swap(array, lambda b, g: (b ^ 2) * grp + g if b & 1 else b * grp + (g ^ 1))

    own = gather(table, row_ids, potentials)
    bit = grp // 2
    while bit > 4:
        own = pack([own, grp_bit(own, bit)])
        bit //= 2
    near = grp_bit(own, 2)
    far = grp_bit(own, 4)
    state = visit([own, core(own)], count, centroids, None, scale)
    pair = pack([own, near])
    x_pair = one_way(pair)
    state = visit([near, core(near)], count, centroids, state, scale)
    y_pair = other_way(pair)
    both = grp_bit(far, 2)
    state = visit([far, core(far)], count, centroids, state, scale)
    xy_pair = other_way(x_pair)
    state = visit([x_pair, core(x_pair)], count, centroids, state, scale)
    late = pack([far, both])
    x_late = one_way(late)
    y_late = other_way(late)
    state = visit([y_pair, core(y_pair), both, core(both)], count, centroids, state, scale)
    xy_late = other_way(x_late)
    state = visit([xy_pair, core(xy_pair)], count, centroids, state, scale)
    state = visit([x_late, core(x_late), y_late, core(y_late)], count, centroids, state, scale)
    means, potential = visit([xy_late, core(xy_late)], count, centroids, state, scale, balance)
    return means, potential.reshape(balance.shape)


def solution(mesh):
    placed = (
        P(AXES, None),
        P(AXES),
        P(AXES),
        P(AXES, None),
        P(AXES),
    )
    return jax.shard_map(
        body,
        mesh=mesh,
        in_specs=placed,
        out_specs=(P(AXES, None), P(AXES)),
        check_vma=False,
    )
```

```python
import functools
import math

import jax
import jax.numpy as jnp
from jax import lax
from jax.experimental import pallas as pl
from jax.experimental.pallas import tpu as pltpu
from jax.sharding import PartitionSpec as P

BF16, F32 = jnp.bfloat16, jnp.float32
AXES = ("blk", "grp")
EXTRA = 16
LANES = 128
VMEM = pl.BlockSpec(memory_space=pltpu.VMEM)
NT = (((1,), (1,)), ((), ()))


def in_vmem(array):
    return pltpu.with_memory_space_constraint(array, pltpu.VMEM)


def eye():
    shape = (LANES, LANES)
    return lax.broadcasted_iota(jnp.int32, shape, 0) == lax.broadcasted_iota(jnp.int32, shape, 1)


def to_row(column):
    return jnp.sum(jnp.where(eye(), column, 0.0), axis=0, keepdims=True)


def to_column(row):
    return jnp.sum(jnp.where(eye(), row, 0.0), axis=1, keepdims=True)


def gather_kernel(table_ref, ids_ref, pots_ref, out_ref, held_ref, ids_held, pots_held, sems):
    records, width = table_ref.shape
    count = ids_ref.shape[1]
    step = 512
    parts = [pl.ds(first, step) for first in range(0, records, step)]
    copies = [pltpu.make_async_copy(ids_ref, ids_held, sems.at[0]), pltpu.make_async_copy(pots_ref, pots_held, sems.at[1])]
    copies += [pltpu.make_async_copy(table_ref.at[p, :], held_ref.at[p, :], sems.at[i + 2]) for i, p in enumerate(parts)]
    for copy in copies:
        copy.start()
    copies[0].wait()
    column = to_column(ids_held[...].astype(F32)).astype(jnp.int32)
    rows = jnp.zeros((count, width), F32)
    for i, copy in enumerate(copies[2:]):
        spot = lax.broadcasted_iota(jnp.int32, (count, step), 1) + i * step
        pick = jnp.where(spot == column, 1.0, 0.0).astype(BF16)
        copy.wait()
        rows += jnp.dot(pick, held_ref[i * step : (i + 1) * step, :], preferred_element_type=F32)
    norm = to_row(jnp.sum(jnp.square(rows), axis=1, keepdims=True))
    copies[1].wait()
    term = pots_held[...].astype(F32) * (width / 2) - 0.5 * norm
    high = term.astype(BF16).astype(F32)
    middle = (term - high).astype(BF16).astype(F32)
    low = term - high - middle
    line = lax.broadcasted_iota(jnp.int32, (EXTRA, LANES), 0)
    split = jnp.where(line == 0, high, jnp.where(line == 1, middle, jnp.where(line == 2, low, 0.0)))
    out_ref[0:count, :] = rows.astype(BF16)
    out_ref[count:, :] = jnp.zeros((EXTRA, width), BF16)
    out_ref[count:, 0:LANES] = split.astype(BF16)


def gather(table, row_ids, potentials):
    count, (records, width) = row_ids.shape[0], table.shape
    args = [table, row_ids.reshape(1, count), potentials.reshape(1, count)]
    return pl.pallas_call(
        gather_kernel,
        out_shape=pltpu.VMEM((count + EXTRA, width), BF16),
        in_specs=[pl.BlockSpec(memory_space=pltpu.HBM)] * 3,
        out_specs=VMEM,
        scratch_shapes=[
            pltpu.VMEM((records, width), BF16),
            pltpu.VMEM((1, count), jnp.int32),
            pltpu.VMEM((1, count), BF16),
            pltpu.SemaphoreType.DMA((records // 512 + 2,)),
        ],
        compiler_params=pltpu.CompilerParams(vmem_limit_bytes=16 << 20),
        name="gather",
    )(*[pltpu.with_memory_space_constraint(a, pltpu.HBM) for a in args])


def pieces(refs, count):
    rows, terms = [], []
    for ref in refs:
        for first in range(0, ref.shape[0], count + EXTRA):
            rows.append(ref[first : first + count, :])
            extra = ref[first + count : first + count + EXTRA, 0:LANES].astype(F32)
            terms.append(jnp.sum(extra, axis=0, keepdims=True))
    return rows, terms


BLOCK=512
def visit_kernel(shards, count, block, chunk, first, last, scale, *refs):
    shard_refs, refs = refs[:shards], refs[shards:]
    centres_ref, refs = refs[0], refs[1:]
    if first:
        source_ref, centres_ref, load_sems, refs = centres_ref, refs[-2], refs[-1], refs[:-2]
    state_in, refs = (None, refs) if first else (refs[:3], refs[3:])
    if last:
        (centre_ref, balance_ref), refs = refs[:2], refs[2:]
        means_ref, potential_ref, held_ref, sems = refs
    width = centres_ref.shape[1]
    alpha = math.log2(math.e) * 2.0 * scale / width
    rows, terms = pieces(shard_refs, count)
    per = max(1, chunk // count)
    groups = [
        (jnp.concatenate(rows[i : i + per], axis=0), jnp.concatenate(terms[i : i + per], axis=1))
        for i in range(0, len(rows), per)
    ]
    acc_ref = held_ref if last else refs[2]


    total = centres_ref.shape[0]
    units = [(j, g) for j in range(total // block) for g in range(len(groups))]
    carry = {}

    def scores(u):
        j, g = u
        at = slice(j * block, (j + 1) * block)
        return lax.dot_general(centres_ref[at, :], groups[g][0], NT, preferred_element_type=F32) + groups[g][1]

    def soft(u, shifted):
        j, g = u
        at = slice(j * block, (j + 1) * block)
        if g == 0:
            old = None if first else state_in[0][at, :]
            mass = None if first else state_in[1][at, :]
        else:
            old, mass = carry[j]
        lanes = [slice(f, f + LANES) for f in range(0, shifted.shape[1], LANES)]
        top = jnp.broadcast_to(jnp.max(shifted, axis=1, keepdims=True), (block, LANES))
        shrink = None
        if old is not None:
            top = jnp.maximum(old, top)
            shrink = jnp.exp2((old - top) * alpha)
            mass = mass * shrink
        parts = []
        for lane in lanes:
            expd = jnp.exp2((shifted[:, lane] - top) * alpha)
            mass = expd if mass is None else mass + expd
            parts.append(expd.astype(BF16))
        carry[j] = (top, mass)
        return jnp.concatenate(parts, axis=1), shrink

    def weigh(u, expd, shrink):
        j, g = u
        at = slice(j * block, (j + 1) * block)
        numer = jnp.dot(expd, groups[g][0], preferred_element_type=F32)
        acc_in = acc_ref if g else (None if first else state_in[2])
        done = g == len(groups) - 1
        if done:
            top, mass = carry[j]
            if last:
                total_mass = jnp.broadcast_to(jnp.sum(mass, axis=1, keepdims=True), (block, LANES))
                inverse = 1.0 / total_mass
                for i in range(block // LANES):
                    part = slice(i * LANES, (i + 1) * LANES)
                    k = j * (block // LANES) + i
                    line = slice(k, k + 1)
                    peak = (scale / width) * (2.0 * to_row(top[part]) - centre_ref[line, :])
                    potential_ref[line, :] = (
                        jnp.log(balance_ref[line, :]) - peak - jnp.log(to_row(total_mass[part]))
                    ) / scale
            else:
                if j == 0:
                    refs[3][...] = top[0:8, :]
                refs[0][at, :] = top
                refs[1][at, :] = mass
        for f in range(0, width, LANES):
            lane = slice(f, f + LANES)
            value = numer[:, lane]
            if acc_in is not None:
                value = acc_in[at, lane] * shrink + value
            if done and last:
                value = value * inverse
            acc_ref[at, lane] = value
        if done and last:
            out_copy(j).start()

    def out_copy(j):
        at = pl.ds(j * block, block)
        return pltpu.make_async_copy(held_ref.at[at, :], means_ref.at[at, :], sems.at[j])

    def load(j):
        at = pl.ds(j * block, block)
        return pltpu.make_async_copy(source_ref.at[at, :], centres_ref.at[at, :], load_sems.at[j])

    if first:
        for j in range(total // block):
            load(j).start()
        for j in range(total // block):
            load(j).wait()
        for i in range(total // LANES):
            centre = jnp.sum(jnp.square(centres_ref[i * LANES : (i + 1) * LANES, :].astype(F32)), axis=1, keepdims=True)
            refs[4][i : i + 1, :] = to_row(centre)

    ahead = scores(units[0])
    for i, u in enumerate(units):
        now = ahead
        if i + 1 < len(units):
            ahead = scores(units[i + 1])
        weigh(u, *soft(u, now))
    if last:
        for j in range(total // block):
            out_copy(j).wait()


def visit(shards, count, centroids, state, scale, balance=None, chunk=1024, cost=0.4):
    total, width = centroids.shape
    block = min(1024, total)
    first, last = state is None, balance is not None
    number = sum(s.shape[0] // (count + EXTRA) for s in shards)
    lines = (total // LANES, LANES)
    scratch = []
    if last:
        out_shape = [jax.ShapeDtypeStruct((total, width), F32), jax.ShapeDtypeStruct(lines, F32)]
        out_specs = [pl.BlockSpec(memory_space=pltpu.HBM), VMEM]
        scratch = [pltpu.VMEM((total, width), F32), pltpu.SemaphoreType.DMA((total // block,))]
    else:
        shapes = [(total, LANES), (total, LANES), (total, width), (8, LANES)] + ([lines] if first else [])
        out_shape = [pltpu.VMEM(shape, F32) for shape in shapes]
        if first:
            out_shape.append(pltpu.VMEM((total, width), BF16))
            scratch = [pltpu.SemaphoreType.DMA((total // block,))]
        out_specs = [VMEM] * len(out_shape)
    args = [in_vmem(s) for s in shards]
    args.append(pltpu.with_memory_space_constraint(centroids, pltpu.HBM) if first else in_vmem(state[5]))
    aliases = {}
    if not first:
        if not last:
            aliases = {len(args) + i: i for i in range(3)}
        args += [in_vmem(s) for s in state[:3]]
    if last:
        args += [in_vmem(state[4]), balance.reshape(lines)]
    rows = number * count
    out = pl.pallas_call(
        functools.partial(visit_kernel, len(shards), count, block, chunk, first, last, scale),
        out_shape=tuple(out_shape),
        in_specs=[pl.BlockSpec(memory_space=pltpu.HBM) if first and i == len(shards) else VMEM for i in range(len(args))],
        out_specs=tuple(out_specs),
        scratch_shapes=scratch,
        input_output_aliases=aliases,
        compiler_params=pltpu.CompilerParams(vmem_limit_bytes=40 << 20),
        cost_estimate=pl.CostEstimate(flops=int(cost * 4 * rows * total * width), bytes_accessed=1024, transcendentals=0),
        name="visit",
    )(*args)
    return out if first or last else (*out, *state[4:])


def joined_kernel(*refs):
    out_ref, first = refs[-1], 0
    for ref in refs[1:-1]:
        out_ref[first : first + ref.shape[0], :] = ref[...]
        first += ref.shape[0]


def joined(parts, token):
    rows = sum(p.shape[0] for p in parts)
    return pl.pallas_call(
        joined_kernel,
        out_shape=pltpu.VMEM((rows, parts[0].shape[1]), BF16),
        in_specs=[VMEM] * (len(parts) + 1),
        out_specs=VMEM,
        compiler_params=pltpu.CompilerParams(vmem_limit_bytes=16 << 20),
        cost_estimate=pl.CostEstimate(flops=0, bytes_accessed=0, transcendentals=0),
        name="joined",
    )(in_vmem(token), *[in_vmem(p) for p in parts])


def body(table, row_ids, potentials, centroids, balance):
    scale = 1.5 * math.sqrt(table.shape[1])
    count = row_ids.shape[0]
    blk, grp = lax.axis_size("blk"), lax.axis_size("grp")

    def swap(array, flip):
        route = [(i, flip(i // grp, i % grp)) for i in range(blk * grp)]
        return lax.ppermute(array, AXES, route)

    def core(array):
        return swap(array, lambda b, g: (b ^ 1) * grp + g)

    def grp_bit(array, bit):
        return swap(array, lambda b, g: b * grp + (g ^ bit))

    def one_way(array):
        return swap(array, lambda b, g: b * grp + (g ^ 1) if b & 1 else (b ^ 2) * grp + g)

    def other_way(array):
        return swap(array, lambda b, g: (b ^ 2) * grp + g if b & 1 else b * grp + (g ^ 1))

    own = gather(table, row_ids, potentials)
    bit = grp // 2
    while bit > 4:
        own = jnp.concatenate([own, grp_bit(own, bit)], axis=0)
        bit //= 2
    look = functools.partial(visit, count=count, centroids=centroids, scale=scale)
    far = grp_bit(own, 4)
    near = grp_bit(own, 2)
    state = look([own, core(own)], state=None, cost=0.01)
    t = state[3]
    a = one_way(joined([own], t))
    near_core = core(joined([near], t))
    two = joined([near, far], t)
    a_two = one_way(two)
    both = grp_bit(joined([far], t), 2)
    far_core = core(joined([far], t))
    state = look([near, far, near_core, far_core], state=state)
    t = state[3]
    b = other_way(joined([own, a], t))
    b_four = other_way(joined([two, a_two], t))
    a_both = one_way(joined([both], t))
    second_core = core(joined([a, a_two, both], t))
    state = look([a, a_two, both, second_core], state=state)
    t = state[3]
    b_two = other_way(joined([both, a_both], t))
    third_core = core(joined([b, a_both], t))
    state = look([b, a_both, third_core], state=state)
    t = state[3]
    b_four_core = core(joined([b_four], t))
    b_two_core = core(joined([b_two], t))
    state = look([b_four, b_two], state=state)
    means, potential = look([b_four_core, b_two_core], state=state, balance=balance)
    return means, potential.reshape(balance.shape)


def solution(mesh):
    placed = (
        P(AXES, None),
        P(AXES),
        P(AXES),
        P(AXES, None),
        P(AXES),
    )
    return jax.shard_map(
        body,
        mesh=mesh,
        in_specs=placed,
        out_specs=(P(AXES, None), P(AXES)),
        check_vma=False,
    )
```

```python
import functools
import math

import jax
import jax.numpy as jnp
from jax import lax
from jax.experimental import pallas as pl
from jax.experimental.pallas import tpu as pltpu
from jax.sharding import PartitionSpec as P

BF16, F32 = jnp.bfloat16, jnp.float32
AXES = ("blk", "grp")
EXTRA = 16
LANES = 128
VMEM = pl.BlockSpec(memory_space=pltpu.VMEM)
NT = (((1,), (1,)), ((), ()))


def in_vmem(array):
    return pltpu.with_memory_space_constraint(array, pltpu.VMEM)


def eye():
    shape = (LANES, LANES)
    return lax.broadcasted_iota(jnp.int32, shape, 0) == lax.broadcasted_iota(jnp.int32, shape, 1)


def to_row(column):
    return jnp.sum(jnp.where(eye(), column, 0.0), axis=0, keepdims=True)


def to_column(row):
    return jnp.sum(jnp.where(eye(), row, 0.0), axis=1, keepdims=True)


def gather_kernel(table_ref, ids_ref, pots_ref, out_ref, held_ref, ids_held, pots_held, sems):
    records, width = table_ref.shape
    count = ids_ref.shape[1]
    step = 512
    parts = [pl.ds(first, step) for first in range(0, records, step)]
    copies = [pltpu.make_async_copy(ids_ref, ids_held, sems.at[0]), pltpu.make_async_copy(pots_ref, pots_held, sems.at[1])]
    copies += [pltpu.make_async_copy(table_ref.at[p, :], held_ref.at[p, :], sems.at[i + 2]) for i, p in enumerate(parts)]
    for copy in copies:
        copy.start()
    copies[0].wait()
    column = to_column(ids_held[...].astype(F32)).astype(jnp.int32)
    rows = jnp.zeros((count, width), F32)
    for i, copy in enumerate(copies[2:]):
        spot = lax.broadcasted_iota(jnp.int32, (count, step), 1) + i * step
        pick = jnp.where(spot == column, 1.0, 0.0).astype(BF16)
        copy.wait()
        rows += jnp.dot(pick, held_ref[i * step : (i + 1) * step, :], preferred_element_type=F32)
    norm = to_row(jnp.sum(jnp.square(rows), axis=1, keepdims=True))
    copies[1].wait()
    term = pots_held[...].astype(F32) * (width / 2) - 0.5 * norm
    high = term.astype(BF16).astype(F32)
    middle = (term - high).astype(BF16).astype(F32)
    low = term - high - middle
    line = lax.broadcasted_iota(jnp.int32, (EXTRA, LANES), 0)
    split = jnp.where(line == 0, high, jnp.where(line == 1, middle, jnp.where(line == 2, low, 0.0)))
    out_ref[0:count, :] = rows.astype(BF16)
    out_ref[count:, :] = jnp.zeros((EXTRA, width), BF16)
    out_ref[count:, 0:LANES] = split.astype(BF16)


def gather(table, row_ids, potentials):
    count, (records, width) = row_ids.shape[0], table.shape
    args = [table, row_ids.reshape(1, count), potentials.reshape(1, count)]
    return pl.pallas_call(
        gather_kernel,
        out_shape=pltpu.VMEM((count + EXTRA, width), BF16),
        in_specs=[pl.BlockSpec(memory_space=pltpu.HBM)] * 3,
        out_specs=VMEM,
        scratch_shapes=[
            pltpu.VMEM((records, width), BF16),
            pltpu.VMEM((1, count), jnp.int32),
            pltpu.VMEM((1, count), BF16),
            pltpu.SemaphoreType.DMA((records // 512 + 2,)),
        ],
        compiler_params=pltpu.CompilerParams(vmem_limit_bytes=16 << 20),
        name="gather",
    )(*[pltpu.with_memory_space_constraint(a, pltpu.HBM) for a in args])


def pieces(refs, count):
    rows, terms = [], []
    for ref in refs:
        for first in range(0, ref.shape[0], count + EXTRA):
            rows.append(ref[first : first + count, :])
            extra = ref[first + count : first + count + EXTRA, 0:LANES].astype(F32)
            terms.append(jnp.sum(extra, axis=0, keepdims=True))
    return rows, terms


BLOCK=512
def visit_kernel(shards, count, block, chunk, first, last, scale, *refs):
    shard_refs, refs = refs[:shards], refs[shards:]
    centres_ref, refs = refs[0], refs[1:]
    if first:
        source_ref, centres_ref, load_sems, refs = centres_ref, refs[-2], refs[-1], refs[:-2]
    state_in, refs = (None, refs) if first else (refs[:3], refs[3:])
    if last:
        (centre_ref, balance_ref), refs = refs[:2], refs[2:]
        means_ref, potential_ref, held_ref, sems = refs
    width = centres_ref.shape[1]
    alpha = math.log2(math.e) * 2.0 * scale / width
    rows, terms = pieces(shard_refs, count)
    most = max(1, chunk // count)
    per = -(-len(rows) // -(-len(rows) // most))
    groups = [
        (jnp.concatenate(rows[i : i + per], axis=0), jnp.concatenate(terms[i : i + per], axis=1))
        for i in range(0, len(rows), per)
    ]
    acc_ref = held_ref if last else refs[2]


    total = centres_ref.shape[0]
    units = [(j, g) for j in range(total // block) for g in range(len(groups))]
    carry = {}

    def scores(u):
        j, g = u
        at = slice(j * block, (j + 1) * block)
        return lax.dot_general(centres_ref[at, :], groups[g][0], NT, preferred_element_type=F32) + groups[g][1]

    def soft(u, shifted):
        j, g = u
        at = slice(j * block, (j + 1) * block)
        if g == 0:
            old = None if first else state_in[0][at, :]
            mass = None if first else state_in[1][at, :]
        else:
            old, mass = carry[j]
        lanes = [slice(f, f + LANES) for f in range(0, shifted.shape[1], LANES)]
        top = jnp.broadcast_to(jnp.max(shifted, axis=1, keepdims=True), (block, LANES))
        shrink = None
        if old is not None:
            top = jnp.maximum(old, top)
            shrink = jnp.exp2((old - top) * alpha)
            mass = mass * shrink
        parts = []
        for lane in lanes:
            expd = jnp.exp2((shifted[:, lane] - top) * alpha)
            mass = expd if mass is None else mass + expd
            parts.append(expd.astype(BF16))
        carry[j] = (top, mass)
        return jnp.concatenate(parts, axis=1), shrink

    def weigh(u, expd, shrink):
        j, g = u
        at = slice(j * block, (j + 1) * block)
        numer = jnp.dot(expd, groups[g][0], preferred_element_type=F32)
        acc_in = acc_ref if g else (None if first else state_in[2])
        done = g == len(groups) - 1
        if done:
            top, mass = carry[j]
            if last:
                total_mass = jnp.broadcast_to(jnp.sum(mass, axis=1, keepdims=True), (block, LANES))
                inverse = 1.0 / total_mass
                for i in range(block // LANES):
                    part = slice(i * LANES, (i + 1) * LANES)
                    k = j * (block // LANES) + i
                    line = slice(k, k + 1)
                    peak = (scale / width) * (2.0 * to_row(top[part]) - centre_ref[line, :])
                    potential_ref[line, :] = (
                        jnp.log(balance_ref[line, :]) - peak - jnp.log(to_row(total_mass[part]))
                    ) / scale
            else:
                if j == 0:
                    refs[3][...] = top[0:8, :]
                refs[0][at, :] = top
                refs[1][at, :] = mass
        for f in range(0, width, LANES):
            lane = slice(f, f + LANES)
            value = numer[:, lane]
            if acc_in is not None:
                value = acc_in[at, lane] * shrink + value
            if done and last:
                value = value * inverse
            acc_ref[at, lane] = value
        if done and last:
            out_copy(j).start()

    def out_copy(j):
        at = pl.ds(j * block, block)
        return pltpu.make_async_copy(held_ref.at[at, :], means_ref.at[at, :], sems.at[j])

    def load(j):
        at = pl.ds(j * block, block)
        return pltpu.make_async_copy(source_ref.at[at, :], centres_ref.at[at, :], load_sems.at[j])

    if first:
        for j in range(total // block):
            load(j).start()
        for j in range(total // block):
            load(j).wait()
        for i in range(total // LANES):
            centre = jnp.sum(jnp.square(centres_ref[i * LANES : (i + 1) * LANES, :].astype(F32)), axis=1, keepdims=True)
            refs[4][i : i + 1, :] = to_row(centre)

    ahead = scores(units[0])
    for i, u in enumerate(units):
        now = ahead
        if i + 1 < len(units):
            ahead = scores(units[i + 1])
        weigh(u, *soft(u, now))
    if last:
        for j in range(total // block):
            out_copy(j).wait()


def visit(shards, count, centroids, state, scale, balance=None, chunk=1024, cost=0.4):
    total, width = centroids.shape
    block = min(1024, total)
    first, last = state is None, balance is not None
    number = sum(s.shape[0] // (count + EXTRA) for s in shards)
    lines = (total // LANES, LANES)
    scratch = []
    if last:
        out_shape = [jax.ShapeDtypeStruct((total, width), F32), jax.ShapeDtypeStruct(lines, F32)]
        out_specs = [pl.BlockSpec(memory_space=pltpu.HBM), VMEM]
        scratch = [pltpu.VMEM((total, width), F32), pltpu.SemaphoreType.DMA((total // block,))]
    else:
        shapes = [(total, LANES), (total, LANES), (total, width), (8, LANES)] + ([lines] if first else [])
        out_shape = [pltpu.VMEM(shape, F32) for shape in shapes]
        if first:
            out_shape.append(pltpu.VMEM((total, width), BF16))
            scratch = [pltpu.SemaphoreType.DMA((total // block,))]
        out_specs = [VMEM] * len(out_shape)
    args = [in_vmem(s) for s in shards]
    args.append(pltpu.with_memory_space_constraint(centroids, pltpu.HBM) if first else in_vmem(state[5]))
    aliases = {}
    if not first:
        if not last:
            aliases = {len(args) + i: i for i in range(3)}
        args += [in_vmem(s) for s in state[:3]]
    if last:
        args += [in_vmem(state[4]), balance.reshape(lines)]
    rows = number * count
    out = pl.pallas_call(
        functools.partial(visit_kernel, len(shards), count, block, chunk, first, last, scale),
        out_shape=tuple(out_shape),
        in_specs=[pl.BlockSpec(memory_space=pltpu.HBM) if first and i == len(shards) else VMEM for i in range(len(args))],
        out_specs=tuple(out_specs),
        scratch_shapes=scratch,
        input_output_aliases=aliases,
        compiler_params=pltpu.CompilerParams(vmem_limit_bytes=40 << 20),
        cost_estimate=pl.CostEstimate(flops=int(cost * 4 * rows * total * width), bytes_accessed=1024, transcendentals=0),
        name="visit",
    )(*args)
    return out if first or last else (*out, *state[4:])


def joined_kernel(halves, *refs):
    out_ref, first = refs[-1], 0
    for ref, half in zip(refs[1:-1], halves):
        skip = ref.shape[0] // 2 if half else 0
        rows = ref.shape[0] - skip
        out_ref[first : first + rows, :] = ref[skip : skip + rows, :]
        first += rows


def joined(parts, token, halves=()):
    half = [i in halves for i in range(len(parts))]
    rows = sum(p.shape[0] // 2 if h else p.shape[0] for p, h in zip(parts, half))
    return pl.pallas_call(
        functools.partial(joined_kernel, half),
        out_shape=pltpu.VMEM((rows, parts[0].shape[1]), BF16),
        in_specs=[VMEM] * (len(parts) + 1),
        out_specs=VMEM,
        compiler_params=pltpu.CompilerParams(vmem_limit_bytes=16 << 20),
        cost_estimate=pl.CostEstimate(flops=0, bytes_accessed=0, transcendentals=0),
        name="joined",
    )(in_vmem(token), *[in_vmem(p) for p in parts])


def body(table, row_ids, potentials, centroids, balance):
    scale = 1.5 * math.sqrt(table.shape[1])
    count = row_ids.shape[0]
    blk, grp = lax.axis_size("blk"), lax.axis_size("grp")

    def swap(array, flip):
        route = [(i, flip(i // grp, i % grp)) for i in range(blk * grp)]
        return lax.ppermute(array, AXES, route)

    def core(array):
        return swap(array, lambda b, g: (b ^ 1) * grp + g)

    def grp_bit(array, bit):
        return swap(array, lambda b, g: b * grp + (g ^ bit))

    def one_way(array):
        return swap(array, lambda b, g: b * grp + (g ^ 1) if b & 1 else (b ^ 2) * grp + g)

    def other_way(array):
        return swap(array, lambda b, g: (b ^ 2) * grp + g if b & 1 else b * grp + (g ^ 1))

    def first_mix(array):
        return swap(array, lambda b, g: b * grp + (g ^ 2 if b & 1 else g ^ 4))

    def second_mix(array):
        return swap(array, lambda b, g: b * grp + (g ^ 4 if b & 1 else g ^ 2))

    own = gather(table, row_ids, potentials)
    bit = grp // 2
    while bit > 4:
        own = jnp.concatenate([own, grp_bit(own, bit)], axis=0)
        bit //= 2
    look = functools.partial(visit, count=count, centroids=centroids, scale=scale)
    far = grp_bit(own, 4)
    near = grp_bit(own, 2)
    a = one_way(own)
    state = look([own, core(own)], state=None, cost=0.01)
    t = state[3]
    far_on = joined([far], t)
    both = grp_bit(far_on, 2)
    first_core = core(joined([a, near, far], far_on))
    two = joined([near, far], far_on)
    a_two = one_way(two)
    b = other_way(joined([own, a], far_on))
    state = look([a, near, far, first_core], state=state)
    t = state[3]
    both_on = joined([both], t)
    a_both = one_way(both_on)
    b_four = other_way(joined([two, a_two], both_on))
    second_core = core(joined([b, a_two, both], both_on))
    state = look([b, a_two], state=state, cost=3.0)
    t = state[3]
    b_two = other_way(joined([both, a_both], t))
    a_both_core = core(joined([a_both], t))
    state = look([both, second_core, a_both, a_both_core], state=state)
    t = state[3]
    b_four_core = core(joined([b_four], t))
    b_two_core = core(joined([b_two], t))
    state = look([b_four, b_two], state=state)
    means, potential = look([b_four_core, b_two_core], state=state, balance=balance)
    return means, potential.reshape(balance.shape)


def solution(mesh):
    placed = (
        P(AXES, None),
        P(AXES),
        P(AXES),
        P(AXES, None),
        P(AXES),
    )
    return jax.shard_map(
        body,
        mesh=mesh,
        in_specs=placed,
        out_specs=(P(AXES, None), P(AXES)),
        check_vma=False,
    )
```

```python
import functools
import math

import jax
import jax.numpy as jnp
from jax import lax
from jax.experimental import pallas as pl
from jax.experimental.pallas import tpu as pltpu
from jax.sharding import PartitionSpec as P

BF16, F32 = jnp.bfloat16, jnp.float32
AXES = ("blk", "grp")
EXTRA = 16
LANES = 128
OUT = 256
VMEM = pl.BlockSpec(memory_space=pltpu.VMEM)
NT = (((1,), (1,)), ((), ()))


def in_vmem(array):
    return pltpu.with_memory_space_constraint(array, pltpu.VMEM)


def eye():
    shape = (LANES, LANES)
    return lax.broadcasted_iota(jnp.int32, shape, 0) == lax.broadcasted_iota(jnp.int32, shape, 1)


def to_row(column):
    return jnp.sum(jnp.where(eye(), column, 0.0), axis=0, keepdims=True)


def to_column(row):
    return jnp.sum(jnp.where(eye(), row, 0.0), axis=1, keepdims=True)


def gather_kernel(table_ref, ids_ref, pots_ref, out_ref, held_ref, ids_held, pots_held, sems):
    records, width = table_ref.shape
    count = ids_ref.shape[1]
    step = 512
    parts = [pl.ds(first, step) for first in range(0, records, step)]
    copies = [pltpu.make_async_copy(ids_ref, ids_held, sems.at[0]), pltpu.make_async_copy(pots_ref, pots_held, sems.at[1])]
    copies += [pltpu.make_async_copy(table_ref.at[p, :], held_ref.at[p, :], sems.at[i + 2]) for i, p in enumerate(parts)]
    for copy in copies:
        copy.start()
    copies[0].wait()
    column = to_column(ids_held[...].astype(F32)).astype(jnp.int32)
    rows = jnp.zeros((count, width), F32)
    for i, copy in enumerate(copies[2:]):
        spot = lax.broadcasted_iota(jnp.int32, (count, step), 1) + i * step
        pick = jnp.where(spot == column, 1.0, 0.0).astype(BF16)
        copy.wait()
        rows += jnp.dot(pick, held_ref[i * step : (i + 1) * step, :], preferred_element_type=F32)
    norm = to_row(jnp.sum(jnp.square(rows), axis=1, keepdims=True))
    copies[1].wait()
    term = pots_held[...].astype(F32) * (width / 2) - 0.5 * norm
    high = term.astype(BF16).astype(F32)
    middle = (term - high).astype(BF16).astype(F32)
    low = term - high - middle
    line = lax.broadcasted_iota(jnp.int32, (EXTRA, LANES), 0)
    split = jnp.where(line == 0, high, jnp.where(line == 1, middle, jnp.where(line == 2, low, 0.0)))
    out_ref[0:count, :] = rows.astype(BF16)
    out_ref[count:, :] = jnp.zeros((EXTRA, width), BF16)
    out_ref[count:, 0:LANES] = split.astype(BF16)


def gather(table, row_ids, potentials):
    count, (records, width) = row_ids.shape[0], table.shape
    args = [table, row_ids.reshape(1, count), potentials.reshape(1, count)]
    return pl.pallas_call(
        gather_kernel,
        out_shape=pltpu.VMEM((count + EXTRA, width), BF16),
        in_specs=[pl.BlockSpec(memory_space=pltpu.HBM)] * 3,
        out_specs=VMEM,
        scratch_shapes=[
            pltpu.VMEM((records, width), BF16),
            pltpu.VMEM((1, count), jnp.int32),
            pltpu.VMEM((1, count), BF16),
            pltpu.SemaphoreType.DMA((records // 512 + 2,)),
        ],
        compiler_params=pltpu.CompilerParams(vmem_limit_bytes=16 << 20),
        name="gather",
    )(*[pltpu.with_memory_space_constraint(a, pltpu.HBM) for a in args])


def pieces(refs, count):
    rows, terms = [], []
    for ref in refs:
        for first in range(0, ref.shape[0], count + EXTRA):
            rows.append(ref[first : first + count, :])
            extra = ref[first + count : first + count + EXTRA, 0:LANES].astype(F32)
            terms.append(jnp.sum(extra, axis=0, keepdims=True))
    return rows, terms


BLOCK=512
def visit_kernel(shards, count, block, chunk, first, last, scale, *refs):
    shard_refs, refs = refs[:shards], refs[shards:]
    centres_ref, refs = refs[0], refs[1:]
    if first:
        source_ref, centres_ref, load_sems, refs = centres_ref, refs[-2], refs[-1], refs[:-2]
    state_in, refs = (None, refs) if first else (refs[:3], refs[3:])
    if last:
        (centre_ref, balance_ref), refs = refs[:2], refs[2:]
        means_ref, potential_ref, held_ref, sems = refs
    width = centres_ref.shape[1]
    alpha = math.log2(math.e) * 2.0 * scale / width
    rows, terms = pieces(shard_refs, count)
    most = max(1, chunk // count)
    per = -(-len(rows) // -(-len(rows) // most))
    groups = [
        (jnp.concatenate(rows[i : i + per], axis=0), jnp.concatenate(terms[i : i + per], axis=1))
        for i in range(0, len(rows), per)
    ]
    acc_ref = held_ref if last else refs[2]


    total = centres_ref.shape[0]
    units = [(j, g) for j in range(total // block) for g in range(len(groups))]
    carry = {}

    def scores(u):
        j, g = u
        at = slice(j * block, (j + 1) * block)
        return lax.dot_general(centres_ref[at, :], groups[g][0], NT, preferred_element_type=F32) + groups[g][1]

    def soft(u, shifted):
        j, g = u
        at = slice(j * block, (j + 1) * block)
        if g == 0:
            old = None if first else state_in[0][at, :]
            mass = None if first else state_in[1][at, :]
        else:
            old, mass = carry[j]
        lanes = [slice(f, f + LANES) for f in range(0, shifted.shape[1], LANES)]
        top = jnp.broadcast_to(jnp.max(shifted, axis=1, keepdims=True), (block, LANES))
        shrink = None
        if old is not None:
            top = jnp.maximum(old, top)
            shrink = jnp.exp2((old - top) * alpha)
            mass = mass * shrink
        parts = []
        for lane in lanes:
            expd = jnp.exp2((shifted[:, lane] - top) * alpha)
            mass = expd if mass is None else mass + expd
            parts.append(expd.astype(BF16))
        carry[j] = (top, mass)
        return jnp.concatenate(parts, axis=1), shrink

    def weigh(u, expd, shrink):
        j, g = u
        at = slice(j * block, (j + 1) * block)
        numer = jnp.dot(expd, groups[g][0], preferred_element_type=F32)
        acc_in = acc_ref if g else (None if first else state_in[2])
        done = g == len(groups) - 1
        if done:
            top, mass = carry[j]
            if last:
                total_mass = jnp.broadcast_to(jnp.sum(mass, axis=1, keepdims=True), (block, LANES))
                inverse = 1.0 / total_mass
                for i in range(block // LANES):
                    part = slice(i * LANES, (i + 1) * LANES)
                    k = j * (block // LANES) + i
                    line = slice(k, k + 1)
                    peak = (scale / width) * (2.0 * to_row(top[part]) - centre_ref[line, :])
                    potential_ref[line, :] = (
                        jnp.log(balance_ref[line, :]) - peak - jnp.log(to_row(total_mass[part]))
                    ) / scale
            else:
                if j == 0:
                    refs[3][...] = top[0:8, :]
                refs[0][at, :] = top
                refs[1][at, :] = mass
        step = min(OUT, block) if done and last else block
        for r in range(0, block, step):
            here, rows_at = slice(r, r + step), slice(j * block + r, j * block + r + step)
            for f in range(0, width, LANES):
                lane = slice(f, f + LANES)
                value = numer[here, lane]
                if acc_in is not None:
                    value = acc_in[rows_at, lane] * shrink[here] + value
                if done and last:
                    value = value * inverse[here]
                acc_ref[rows_at, lane] = value
            if done and last:
                out_copy((j * block + r) // step).start()

    def out_copy(j):
        at = pl.ds(j * min(OUT, block), min(OUT, block))
        return pltpu.make_async_copy(held_ref.at[at, :], means_ref.at[at, :], sems.at[j])

    def load(j):
        at = pl.ds(j * block, block)
        return pltpu.make_async_copy(source_ref.at[at, :], centres_ref.at[at, :], load_sems.at[j])

    if first:
        for j in range(total // block):
            load(j).start()
        for j in range(total // block):
            load(j).wait()
        for i in range(total // LANES):
            centre = jnp.sum(jnp.square(centres_ref[i * LANES : (i + 1) * LANES, :].astype(F32)), axis=1, keepdims=True)
            refs[4][i : i + 1, :] = to_row(centre)

    ahead = scores(units[0])
    for i, u in enumerate(units):
        now = ahead
        if i + 1 < len(units):
            ahead = scores(units[i + 1])
        weigh(u, *soft(u, now))
    if last:
        for j in range(total // min(OUT, block)):
            out_copy(j).wait()


def visit(shards, count, centroids, state, scale, balance=None, chunk=1024, cost=0.4):
    total, width = centroids.shape
    block = min(1024, total)
    first, last = state is None, balance is not None
    number = sum(s.shape[0] // (count + EXTRA) for s in shards)
    lines = (total // LANES, LANES)
    scratch = []
    if last:
        out_shape = [jax.ShapeDtypeStruct((total, width), F32), jax.ShapeDtypeStruct(lines, F32)]
        out_specs = [pl.BlockSpec(memory_space=pltpu.HBM), VMEM]
        scratch = [pltpu.VMEM((total, width), F32), pltpu.SemaphoreType.DMA((total // min(OUT, block),))]
    else:
        shapes = [(total, LANES), (total, LANES), (total, width), (8, LANES)] + ([lines] if first else [])
        out_shape = [pltpu.VMEM(shape, F32) for shape in shapes]
        if first:
            out_shape.append(pltpu.VMEM((total, width), BF16))
            scratch = [pltpu.SemaphoreType.DMA((total // block,))]
        out_specs = [VMEM] * len(out_shape)
    args = [in_vmem(s) for s in shards]
    args.append(pltpu.with_memory_space_constraint(centroids, pltpu.HBM) if first else in_vmem(state[5]))
    aliases = {}
    if not first:
        if not last:
            aliases = {len(args) + i: i for i in range(3)}
        args += [in_vmem(s) for s in state[:3]]
    if last:
        args += [in_vmem(state[4]), balance.reshape(lines)]
    rows = number * count
    out = pl.pallas_call(
        functools.partial(visit_kernel, len(shards), count, block, chunk, first, last, scale),
        out_shape=tuple(out_shape),
        in_specs=[pl.BlockSpec(memory_space=pltpu.HBM) if first and i == len(shards) else VMEM for i in range(len(args))],
        out_specs=tuple(out_specs),
        scratch_shapes=scratch,
        input_output_aliases=aliases,
        compiler_params=pltpu.CompilerParams(vmem_limit_bytes=40 << 20),
        cost_estimate=pl.CostEstimate(flops=int(cost * 4 * rows * total * width), bytes_accessed=1024, transcendentals=0),
        name="visit",
    )(*args)
    return out if first or last else (*out, *state[4:])


def joined_kernel(halves, *refs):
    out_ref, first = refs[-1], 0
    for ref, half in zip(refs[1:-1], halves):
        skip = ref.shape[0] // 2 if half else 0
        rows = ref.shape[0] - skip
        out_ref[first : first + rows, :] = ref[skip : skip + rows, :]
        first += rows


def joined(parts, token, halves=()):
    half = [i in halves for i in range(len(parts))]
    rows = sum(p.shape[0] // 2 if h else p.shape[0] for p, h in zip(parts, half))
    return pl.pallas_call(
        functools.partial(joined_kernel, half),
        out_shape=pltpu.VMEM((rows, parts[0].shape[1]), BF16),
        in_specs=[VMEM] * (len(parts) + 1),
        out_specs=VMEM,
        compiler_params=pltpu.CompilerParams(vmem_limit_bytes=16 << 20),
        cost_estimate=pl.CostEstimate(flops=0, bytes_accessed=0, transcendentals=0),
        name="joined",
    )(in_vmem(token), *[in_vmem(p) for p in parts])


def body(table, row_ids, potentials, centroids, balance):
    scale = 1.5 * math.sqrt(table.shape[1])
    count = row_ids.shape[0]
    blk, grp = lax.axis_size("blk"), lax.axis_size("grp")

    def swap(array, flip):
        route = [(i, flip(i // grp, i % grp)) for i in range(blk * grp)]
        return lax.ppermute(array, AXES, route)

    def core(array):
        return swap(array, lambda b, g: (b ^ 1) * grp + g)

    def grp_bit(array, bit):
        return swap(array, lambda b, g: b * grp + (g ^ bit))

    def one_way(array):
        return swap(array, lambda b, g: b * grp + (g ^ 1) if b & 1 else (b ^ 2) * grp + g)

    def other_way(array):
        return swap(array, lambda b, g: (b ^ 2) * grp + g if b & 1 else b * grp + (g ^ 1))

    def first_mix(array):
        return swap(array, lambda b, g: b * grp + (g ^ 2 if b & 1 else g ^ 4))

    def second_mix(array):
        return swap(array, lambda b, g: b * grp + (g ^ 4 if b & 1 else g ^ 2))

    own = gather(table, row_ids, potentials)
    bit = grp // 2
    while bit > 4:
        own = jnp.concatenate([own, grp_bit(own, bit)], axis=0)
        bit //= 2
    look = functools.partial(visit, count=count, centroids=centroids, scale=scale)
    far = grp_bit(own, 4)
    near = grp_bit(own, 2)
    a = one_way(own)
    state = look([own, core(own)], state=None, cost=0.01)
    t = state[3]
    far_on = joined([far], t)
    both = grp_bit(far_on, 2)
    first_core = core(joined([a, near, far], far_on))
    two = joined([near, far], far_on)
    a_two = one_way(two)
    b = other_way(joined([own, a], two))
    state = look([a, near, far, first_core], state=state, cost=0.1)
    t = state[3]
    both_on = joined([both], t)
    a_both = one_way(both_on)
    b_four = other_way(joined([two, a_two], both_on))
    second_core = core(joined([b, a_two, both], both_on))
    state = look([b, a_two], state=state, cost=3.0)
    t = state[3]
    b_two = other_way(joined([both, a_both], t))
    a_both_core = core(joined([a_both], t))
    state = look([both, second_core, a_both, a_both_core], state=state, cost=0.4)
    t = state[3]
    b_four_core = core(joined([b_four], t))
    b_two_core = core(joined([b_two], t))
    state = look([b_four, b_two], state=state, cost=1.0)
    means, potential = look([b_four_core, b_two_core], state=state, balance=balance, cost=1.0)
    return means, potential.reshape(balance.shape)


def solution(mesh):
    placed = (
        P(AXES, None),
        P(AXES),
        P(AXES),
        P(AXES, None),
        P(AXES),
    )
    return jax.shard_map(
        body,
        mesh=mesh,
        in_specs=placed,
        out_specs=(P(AXES, None), P(AXES)),
        check_vma=False,
    )
```

```python
import functools
import math

import jax
import jax.numpy as jnp
from jax import lax
from jax.experimental import pallas as pl
from jax.experimental.pallas import tpu as pltpu
from jax.sharding import PartitionSpec as P

BF16, F32 = jnp.bfloat16, jnp.float32
AXES = ("blk", "grp")
EXTRA = 16
LANES = 128
OUT = 128
VMEM = pl.BlockSpec(memory_space=pltpu.VMEM)
NT = (((1,), (1,)), ((), ()))


def in_vmem(array):
    return pltpu.with_memory_space_constraint(array, pltpu.VMEM)


def eye():
    shape = (LANES, LANES)
    return lax.broadcasted_iota(jnp.int32, shape, 0) == lax.broadcasted_iota(jnp.int32, shape, 1)


def to_row(column):
    return jnp.sum(jnp.where(eye(), column, 0.0), axis=0, keepdims=True)


def to_column(row):
    return jnp.sum(jnp.where(eye(), row, 0.0), axis=1, keepdims=True)


def gather_kernel(table_ref, ids_ref, pots_ref, out_ref, held_ref, ids_held, pots_held, sems):
    records, width = table_ref.shape
    count = ids_ref.shape[1]
    step = 512
    parts = [pl.ds(first, step) for first in range(0, records, step)]
    copies = [pltpu.make_async_copy(ids_ref, ids_held, sems.at[0]), pltpu.make_async_copy(pots_ref, pots_held, sems.at[1])]
    copies += [pltpu.make_async_copy(table_ref.at[p, :], held_ref.at[p, :], sems.at[i + 2]) for i, p in enumerate(parts)]
    for copy in copies:
        copy.start()
    copies[0].wait()
    column = to_column(ids_held[...].astype(F32)).astype(jnp.int32)
    rows = jnp.zeros((count, width), F32)
    for i, copy in enumerate(copies[2:]):
        spot = lax.broadcasted_iota(jnp.int32, (count, step), 1) + i * step
        pick = jnp.where(spot == column, 1.0, 0.0).astype(BF16)
        copy.wait()
        rows += jnp.dot(pick, held_ref[i * step : (i + 1) * step, :], preferred_element_type=F32)
    norm = to_row(jnp.sum(jnp.square(rows), axis=1, keepdims=True))
    copies[1].wait()
    term = pots_held[...].astype(F32) * (width / 2) - 0.5 * norm
    high = term.astype(BF16).astype(F32)
    middle = (term - high).astype(BF16).astype(F32)
    low = term - high - middle
    line = lax.broadcasted_iota(jnp.int32, (EXTRA, LANES), 0)
    split = jnp.where(line == 0, high, jnp.where(line == 1, middle, jnp.where(line == 2, low, 0.0)))
    out_ref[0:count, :] = rows.astype(BF16)
    out_ref[count:, :] = jnp.zeros((EXTRA, width), BF16)
    out_ref[count:, 0:LANES] = split.astype(BF16)


def gather(table, row_ids, potentials):
    count, (records, width) = row_ids.shape[0], table.shape
    args = [table, row_ids.reshape(1, count), potentials.reshape(1, count)]
    return pl.pallas_call(
        gather_kernel,
        out_shape=pltpu.VMEM((count + EXTRA, width), BF16),
        in_specs=[pl.BlockSpec(memory_space=pltpu.HBM)] * 3,
        out_specs=VMEM,
        scratch_shapes=[
            pltpu.VMEM((records, width), BF16),
            pltpu.VMEM((1, count), jnp.int32),
            pltpu.VMEM((1, count), BF16),
            pltpu.SemaphoreType.DMA((records // 512 + 2,)),
        ],
        compiler_params=pltpu.CompilerParams(vmem_limit_bytes=16 << 20),
        name="gather",
    )(*[pltpu.with_memory_space_constraint(a, pltpu.HBM) for a in args])


def pieces(refs, count):
    rows, terms = [], []
    for ref in refs:
        for first in range(0, ref.shape[0], count + EXTRA):
            rows.append(ref[first : first + count, :])
            extra = ref[first + count : first + count + EXTRA, 0:LANES].astype(F32)
            terms.append(jnp.sum(extra, axis=0, keepdims=True))
    return rows, terms


BLOCK=512
def visit_kernel(shards, count, block, chunk, first, last, scale, *refs):
    shard_refs, refs = refs[:shards], refs[shards:]
    centres_ref, refs = refs[0], refs[1:]
    if first:
        source_ref, centres_ref, load_sems, refs = centres_ref, refs[-2], refs[-1], refs[:-2]
    state_in, refs = (None, refs) if first else (refs[:3], refs[3:])
    if last:
        (centre_ref, balance_ref), refs = refs[:2], refs[2:]
        means_ref, potential_ref, held_ref, sems = refs
    width = centres_ref.shape[1]
    alpha = math.log2(math.e) * 2.0 * scale / width
    rows, terms = pieces(shard_refs, count)
    most = max(1, chunk // count)
    per = -(-len(rows) // -(-len(rows) // most))
    groups = [
        (jnp.concatenate(rows[i : i + per], axis=0), jnp.concatenate(terms[i : i + per], axis=1))
        for i in range(0, len(rows), per)
    ]
    acc_ref = held_ref if last else refs[2]


    total = centres_ref.shape[0]
    units = [(j, g) for j in range(total // block) for g in range(len(groups))]
    carry = {}

    def scores(u):
        j, g = u
        at = slice(j * block, (j + 1) * block)
        return lax.dot_general(centres_ref[at, :], groups[g][0], NT, preferred_element_type=F32) + groups[g][1]

    def soft(u, shifted):
        j, g = u
        at = slice(j * block, (j + 1) * block)
        if g == 0:
            old = None if first else state_in[0][at, :]
            mass = None if first else state_in[1][at, :]
        else:
            old, mass = carry[j]
        lanes = [slice(f, f + LANES) for f in range(0, shifted.shape[1], LANES)]
        top = jnp.broadcast_to(jnp.max(shifted, axis=1, keepdims=True), (block, LANES))
        shrink = None
        if old is not None:
            top = jnp.maximum(old, top)
            shrink = jnp.exp2((old - top) * alpha)
            mass = mass * shrink
        parts = []
        for lane in lanes:
            expd = jnp.exp2((shifted[:, lane] - top) * alpha)
            mass = expd if mass is None else mass + expd
            parts.append(expd.astype(BF16))
        carry[j] = (top, mass)
        return jnp.concatenate(parts, axis=1), shrink

    def weigh(u, expd, shrink):
        j, g = u
        at = slice(j * block, (j + 1) * block)
        numer = jnp.dot(expd, groups[g][0], preferred_element_type=F32)
        acc_in = acc_ref if g else (None if first else state_in[2])
        done = g == len(groups) - 1
        if done:
            top, mass = carry[j]
            if last:
                total_mass = jnp.broadcast_to(jnp.sum(mass, axis=1, keepdims=True), (block, LANES))
                inverse = 1.0 / total_mass
                for i in range(block // LANES):
                    part = slice(i * LANES, (i + 1) * LANES)
                    k = j * (block // LANES) + i
                    line = slice(k, k + 1)
                    peak = (scale / width) * (2.0 * to_row(top[part]) - centre_ref[line, :])
                    potential_ref[line, :] = (
                        jnp.log(balance_ref[line, :]) - peak - jnp.log(to_row(total_mass[part]))
                    ) / scale
            else:
                if j == 0:
                    refs[3][...] = top[0:8, :]
                refs[0][at, :] = top
                refs[1][at, :] = mass
        step = min(OUT, block) if done and last else block
        for r in range(0, block, step):
            here, rows_at = slice(r, r + step), slice(j * block + r, j * block + r + step)
            for f in range(0, width, LANES):
                lane = slice(f, f + LANES)
                value = numer[here, lane]
                if acc_in is not None:
                    value = acc_in[rows_at, lane] * shrink[here] + value
                if done and last:
                    value = value * inverse[here]
                acc_ref[rows_at, lane] = value
            if done and last:
                out_copy((j * block + r) // step).start()

    def out_copy(j):
        at = pl.ds(j * min(OUT, block), min(OUT, block))
        return pltpu.make_async_copy(held_ref.at[at, :], means_ref.at[at, :], sems.at[j])

    def load(j):
        at = pl.ds(j * block, block)
        return pltpu.make_async_copy(source_ref.at[at, :], centres_ref.at[at, :], load_sems.at[j])

    if first:
        for j in range(total // block):
            load(j).start()
        for j in range(total // block):
            load(j).wait()
        for i in range(total // LANES):
            centre = jnp.sum(jnp.square(centres_ref[i * LANES : (i + 1) * LANES, :].astype(F32)), axis=1, keepdims=True)
            refs[4][i : i + 1, :] = to_row(centre)

    ahead = scores(units[0])
    for i, u in enumerate(units):
        now = ahead
        if i + 1 < len(units):
            ahead = scores(units[i + 1])
        weigh(u, *soft(u, now))
    if last:
        for j in range(total // min(OUT, block)):
            out_copy(j).wait()


def visit(shards, count, centroids, state, scale, balance=None, chunk=1024, cost=0.4):
    total, width = centroids.shape
    block = min(1024, total)
    first, last = state is None, balance is not None
    number = sum(s.shape[0] // (count + EXTRA) for s in shards)
    lines = (total // LANES, LANES)
    scratch = []
    if last:
        out_shape = [jax.ShapeDtypeStruct((total, width), F32), jax.ShapeDtypeStruct(lines, F32)]
        out_specs = [pl.BlockSpec(memory_space=pltpu.HBM), VMEM]
        scratch = [pltpu.VMEM((total, width), F32), pltpu.SemaphoreType.DMA((total // min(OUT, block),))]
    else:
        shapes = [(total, LANES), (total, LANES), (total, width), (8, LANES)] + ([lines] if first else [])
        out_shape = [pltpu.VMEM(shape, F32) for shape in shapes]
        if first:
            out_shape.append(pltpu.VMEM((total, width), BF16))
            scratch = [pltpu.SemaphoreType.DMA((total // block,))]
        out_specs = [VMEM] * len(out_shape)
    args = [in_vmem(s) for s in shards]
    args.append(pltpu.with_memory_space_constraint(centroids, pltpu.HBM) if first else in_vmem(state[5]))
    aliases = {}
    if not first:
        if not last:
            aliases = {len(args) + i: i for i in range(3)}
        args += [in_vmem(s) for s in state[:3]]
    if last:
        args += [in_vmem(state[4]), balance.reshape(lines)]
    rows = number * count
    out = pl.pallas_call(
        functools.partial(visit_kernel, len(shards), count, block, chunk, first, last, scale),
        out_shape=tuple(out_shape),
        in_specs=[pl.BlockSpec(memory_space=pltpu.HBM) if first and i == len(shards) else VMEM for i in range(len(args))],
        out_specs=tuple(out_specs),
        scratch_shapes=scratch,
        input_output_aliases=aliases,
        compiler_params=pltpu.CompilerParams(vmem_limit_bytes=40 << 20),
        cost_estimate=pl.CostEstimate(flops=int(cost * 4 * rows * total * width), bytes_accessed=1024, transcendentals=0),
        name="visit",
    )(*args)
    return out if first or last else (*out, *state[4:])


def joined_kernel(halves, *refs):
    out_ref, first = refs[-1], 0
    for ref, half in zip(refs[1:-1], halves):
        skip = ref.shape[0] // 2 if half else 0
        rows = ref.shape[0] - skip
        out_ref[first : first + rows, :] = ref[skip : skip + rows, :]
        first += rows


def joined(parts, token, halves=()):
    half = [i in halves for i in range(len(parts))]
    rows = sum(p.shape[0] // 2 if h else p.shape[0] for p, h in zip(parts, half))
    return pl.pallas_call(
        functools.partial(joined_kernel, half),
        out_shape=pltpu.VMEM((rows, parts[0].shape[1]), BF16),
        in_specs=[VMEM] * (len(parts) + 1),
        out_specs=VMEM,
        compiler_params=pltpu.CompilerParams(vmem_limit_bytes=16 << 20),
        cost_estimate=pl.CostEstimate(flops=0, bytes_accessed=0, transcendentals=0),
        name="joined",
    )(in_vmem(token), *[in_vmem(p) for p in parts])


def body(table, row_ids, potentials, centroids, balance):
    scale = 1.5 * math.sqrt(table.shape[1])
    count = row_ids.shape[0]
    blk, grp = lax.axis_size("blk"), lax.axis_size("grp")

    def swap(array, flip):
        route = [(i, flip(i // grp, i % grp)) for i in range(blk * grp)]
        return lax.ppermute(array, AXES, route)

    def core(array):
        return swap(array, lambda b, g: (b ^ 1) * grp + g)

    def grp_bit(array, bit):
        return swap(array, lambda b, g: b * grp + (g ^ bit))

    def one_way(array):
        return swap(array, lambda b, g: b * grp + (g ^ 1) if b & 1 else (b ^ 2) * grp + g)

    def other_way(array):
        return swap(array, lambda b, g: (b ^ 2) * grp + g if b & 1 else b * grp + (g ^ 1))

    def first_mix(array):
        return swap(array, lambda b, g: b * grp + (g ^ 2 if b & 1 else g ^ 4))

    def second_mix(array):
        return swap(array, lambda b, g: b * grp + (g ^ 4 if b & 1 else g ^ 2))

    own = gather(table, row_ids, potentials)
    bit = grp // 2
    while bit > 4:
        own = jnp.concatenate([own, grp_bit(own, bit)], axis=0)
        bit //= 2
    look = functools.partial(visit, count=count, centroids=centroids, scale=scale)
    far = grp_bit(own, 4)
    near = grp_bit(own, 2)
    a = one_way(own)
    state = look([own, core(own)], state=None, cost=0.01)
    t = state[3]
    far_on = joined([far], t)
    both = grp_bit(far_on, 2)
    first_core = core(joined([a, near, far], far_on))
    two = joined([near, far], far_on)
    a_two = one_way(two)
    b = other_way(joined([own, a], two))
    state = look([a, near, far, first_core], state=state, cost=0.1)
    t = state[3]
    both_on = joined([both], t)
    a_both = one_way(both_on)
    b_four = other_way(joined([two, a_two], both_on))
    second_core = core(joined([b, a_two, both], both_on))
    state = look([b, a_two], state=state, cost=3.0)
    t = state[3]
    b_two = other_way(joined([both, a_both], t))
    a_both_core = core(joined([a_both], t))
    state = look([both, second_core, a_both, a_both_core], state=state, cost=0.4)
    t = state[3]
    b_four_core = core(joined([b_four], t))
    b_two_core = core(joined([b_two], t))
    state = look([b_four, b_two], state=state, cost=1.0)
    means, potential = look([b_four_core, b_two_core], state=state, balance=balance, cost=1.0)
    return means, potential.reshape(balance.shape)


def solution(mesh):
    placed = (
        P(AXES, None),
        P(AXES),
        P(AXES),
        P(AXES, None),
        P(AXES),
    )
    return jax.shard_map(
        body,
        mesh=mesh,
        in_specs=placed,
        out_specs=(P(AXES, None), P(AXES)),
        check_vma=False,
    )
```
